256 devices in a mesh: grp: 16 (over z, core), seq: 16 (over x, y).
Axes of the slice: x: 4, y: 4, z: 8, core: 2. Of those that a mesh axis runs over, the one named last changes fastest.
Arguments:
- inputs: bfloat16 [16, 2048, 5120], P('grp', 'seq'), may hold values from -6 to 6
- queries: bfloat16 [16, 2048, 4096], P('grp', 'seq'), may hold values from -600 to 600, as said below
- keys: bfloat16 [16, 2048, 512], P('grp', 'seq'), may hold values from -6 to 6, as said below
- values: bfloat16 [16, 2048, 512], P('grp', 'seq'), may hold values from -6 to 6
- outputs: bfloat16 [16, 2048, 4096], P('grp', 'seq'), may hold values from -6 to 6
- upstream: bfloat16 [16, 2048, 4096], P('grp', 'seq'), may hold values from -6 to 6
- lengths: int32 [16, 8], P('grp'), may hold values from 1 to 1024, 2048 in all within a row
- tenants: int32 [16, 8], P('grp'), may hold values from 0 to 7
- adapter_down_maps: bfloat16 [5120, 128], replicated, may hold values from -0.078125 to 0.078125
- adapter_up_maps: bfloat16 [128, 512], replicated, may hold values from -1.5 to 1.5
Outputs:
- queries_gradient: bfloat16 [16, 2048, 4096], P('grp', 'seq')
- keys_gradient: bfloat16 [16, 2048, 512], P('grp', 'seq')
- values_gradient: bfloat16 [16, 2048, 512], P('grp', 'seq')
- down_map_gradient: float32 [5120, 128], replicated
- up_map_gradient: float32 [128, 512], replicated
The draws below stay inside these ranges and needn't reach their ends.
Inputs may be any that keep to these rules, and one draw needn't show every extreme that they name: `keys`: keys of order one. `queries`: queries of order one or more.
All inputs are finite; a program needn't handle non-finite values.
Results may differ from the reference program's by a relative error of at most 0.015.
Values may be sent and summed in bfloat16 or wider, within the bound.
No kernel may reach another device: no remote copies, remote signals or barrier semaphores. Data moves between devices by JAX's collectives and lax.ppermute only.
A program may use at most 64 MiB of HBM per device.

```python
import math
import jax
import jax.numpy as jnp
import numpy as np
from jax import lax

MODEL_WIDTH = 5120
QUERY_HEADS = 32
KEY_VALUE_HEADS = 4
HEAD_SIZE = 128
ADAPTER_RANK = 16
TENANT_COUNT = 8
DOCS = 8
STREAM_POSITIONS = 2048
STREAM_COUNT = 16
MOST = 1024
N_SEQ = 16


def key_base(key):
    return jnp.clip(jax.random.normal(key, (STREAM_COUNT, STREAM_POSITIONS, KEY_VALUE_HEADS, HEAD_SIZE), jnp.float32), -6.0, 6.0)


def draw_keys(key, part):
    base_values = key_base(key)
    backward_result = base_values
    return backward_result.reshape(STREAM_COUNT, STREAM_POSITIONS, KEY_VALUE_HEADS * HEAD_SIZE).astype(jnp.bfloat16)


def draw_queries(key, part):
    key = jax.random.fold_in(key, 5)
    backward_result = jnp.clip(jax.random.normal(key, (STREAM_COUNT, STREAM_POSITIONS, QUERY_HEADS, HEAD_SIZE), jnp.float32), -6.0, 6.0)
    return backward_result.reshape(STREAM_COUNT, STREAM_POSITIONS, QUERY_HEADS * HEAD_SIZE).astype(jnp.bfloat16)


def place_ends(result, own_key, smallest, high):
    place = [jax.random.randint(jax.random.fold_in(own_key, axis), (), 0, length) for axis, length in enumerate(result.shape)]
    widest = result.shape.index(max(result.shape))
    beside = place[:widest] + [(place[widest] + 1) % result.shape[widest]] + place[widest + 1:]
    return result.at[tuple(place)].set(smallest).at[tuple(beside)].set(high)


def steps_of(own_key, shape, split, smallest, top_value):
    def one(axis_at, shards_of):
        heights = jax.random.uniform(jax.random.fold_in(jax.random.fold_in(own_key, 6), axis_at), (shards_of,), jnp.float32, smallest / len(split), top_value / len(split))
        return jnp.repeat(jnp.exp(heights), shape[axis_at] // shards_of).reshape((-1,) + (1,) * (len(shape) - axis_at - 1))

    level = one(*split[0])
    for cut in split[1:]:
        level = level * one(*cut)
    return level


def split_up(number_of, total, reach, slope):
    loads = [(1 << 20) // math.isqrt(grade ** slope) + 1 for grade in range(2, number_of + 1)]
    rest, holding = total - reach - (number_of - 1), [1] * (number_of - 1)
    while rest > 0:
        free = [i for i in range(number_of - 1) if holding[i] < reach]
        whole, remaining = sum([loads[i] for i in free]), rest
        for i in free:
            more = min(reach - holding[i], max(1, remaining * loads[i] // whole), rest)
            holding[i] = holding[i] + more
            rest = rest - more
    return np.array([reach] + holding)


def ragged(stream_key, number_of, total, limit, lean):
    if number_of == 2:
        one = jax.random.randint(stream_key, (), max(1, total - limit), min(limit, total - 1) + 1)
        return jnp.stack([one, total - one])
    sizes = jnp.asarray(split_up(number_of, total, limit, lean), jnp.int32)
    twos = (number_of - 1) // 2
    donor, receiver = sizes[1:1 + 2 * twos:2], sizes[2:2 + 2 * twos:2]
    margin = jnp.minimum(donor - 1, limit - receiver)
    shifted = jax.random.randint(jax.random.fold_in(stream_key, 1), (twos,), 0, 1 << 20) % (margin + 1)
    sizes = sizes.at[1:1 + 2 * twos:2].set(donor - shifted).at[2:2 + 2 * twos:2].set(receiver + shifted)
    return sizes[jax.random.permutation(jax.random.fold_in(stream_key, 2), number_of)]


def noise(rng, shape, deviation, limit, shards=(), kind=jnp.bfloat16):
    drawn = deviation * jax.random.normal(rng, shape, jnp.float32)
    if shards:
        drawn = drawn * steps_of(rng, shape, shards, -0.22, 0.18)
    return jnp.clip(drawn, -limit, limit).astype(kind)


def setup_inputs(seed: int = 0) -> dict:
    splits = jax.random.split(jax.random.key(seed), 11)
    return {
        "inputs": noise(splits[0], (STREAM_COUNT, STREAM_POSITIONS, MODEL_WIDTH), 1.0, 6.0, ((0, 16), (1, 16))),
        "queries": draw_queries(jax.random.fold_in(splits[10], 71), 0),
        "keys": draw_keys(jax.random.fold_in(splits[10], 71), 0),
        "values": noise(splits[3], (STREAM_COUNT, STREAM_POSITIONS, KEY_VALUE_HEADS * HEAD_SIZE), 1.0, 6.0, ((0, 16), (1, 16))),
        "outputs": noise(splits[4], (STREAM_COUNT, STREAM_POSITIONS, QUERY_HEADS * HEAD_SIZE), 1.0, 6.0, ((0, 16), (1, 16))),
        "upstream": noise(splits[5], (STREAM_COUNT, STREAM_POSITIONS, QUERY_HEADS * HEAD_SIZE), 1.0, 6.0, ((0, 16), (1, 16))),
        "lengths": jax.vmap(lambda own: ragged(own, DOCS, STREAM_POSITIONS, MOST, 2))(jax.random.split(splits[6], STREAM_COUNT)).reshape((STREAM_COUNT, DOCS)).astype(jnp.int32),
        "tenants": place_ends(jax.random.randint(splits[7], (STREAM_COUNT, DOCS), 0, TENANT_COUNT), jax.random.fold_in(splits[7], 1), 0, TENANT_COUNT - 1).astype(jnp.int32),
        "adapter_down_maps": noise(splits[8], (MODEL_WIDTH, TENANT_COUNT * ADAPTER_RANK), MODEL_WIDTH ** -0.5, 0.078125),
        "adapter_up_maps": noise(splits[9], (TENANT_COUNT * ADAPTER_RANK, KEY_VALUE_HEADS * HEAD_SIZE), ADAPTER_RANK ** -0.5, 1.5),
    }


adapter_scale = 2.0


def segment_ids(lengths, positions):
    ends = jnp.cumsum(lengths).astype(jnp.int32)
    return jnp.sum((positions[:, None] >= ends[None, :]).astype(jnp.int32), axis=1)


def tenant_ids(segments, tenants):
    docs = jnp.arange(tenants.shape[0], dtype=jnp.int32)
    return jnp.sum(jnp.where(segments[:, None] == docs[None, :], tenants[None, :], 0), axis=1).astype(jnp.int32)


def head_grads(query, upstream, output, key, value_rows, segments):
    scale = HEAD_SIZE ** -0.5
    span = query.shape[0]
    scores = jnp.dot(query, key.T, preferred_element_type=jnp.float32) * scale
    row_indices = jnp.arange(span, dtype=jnp.int32)
    allowed = (segments[:, None] == segments[None, :]) & (row_indices[None, :] <= row_indices[:, None])
    masked = jnp.where(allowed, scores, -jnp.inf)
    top = jnp.max(masked, axis=1, keepdims=True)
    weights = jnp.exp(masked - top)
    prob = weights / jnp.sum(weights, axis=1, keepdims=True)
    delta = jnp.sum(upstream.astype(jnp.float32) * output.astype(jnp.float32), axis=1)
    dprob = jnp.dot(upstream, value_rows.T, preferred_element_type=jnp.float32)
    dscore = (prob * (dprob - delta[:, None])).astype(jnp.bfloat16)
    dquery = (jnp.dot(dscore, key, preferred_element_type=jnp.float32) * scale).astype(jnp.bfloat16)
    key_gradient = jnp.dot(dscore.T, query, preferred_element_type=jnp.float32) * scale
    value_gradient = jnp.dot(prob.astype(jnp.bfloat16).T, upstream, preferred_element_type=jnp.float32)
    return dquery, key_gradient, value_gradient


def partial_sum(gradient_tuple, query_group_size, per_tenant_slot):
    document_runs = jnp.sum(gradient_tuple.reshape(KEY_VALUE_HEADS, query_group_size // per_tenant_slot, per_tenant_slot, STREAM_POSITIONS, HEAD_SIZE), axis=2)
    document_runs = lax.optimization_barrier(document_runs.astype(jnp.bfloat16))
    return jnp.sum(document_runs.astype(jnp.float32), axis=1).astype(jnp.bfloat16)


def reference(inputs, queries, keys, values, outputs, upstream, lengths, tenants, adapter_down_maps, adapter_up_maps):
    query_group_size = QUERY_HEADS // KEY_VALUE_HEADS
    per_tenant_slot = QUERY_HEADS // N_SEQ

    def one_group(items):
        query, key, value_rows, output, grad_out, lens = items
        segments = segment_ids(lens, jnp.arange(STREAM_POSITIONS, dtype=jnp.int32))
        q_heads = query.reshape(STREAM_POSITIONS, QUERY_HEADS, HEAD_SIZE).transpose(1, 0, 2)
        u_heads = grad_out.reshape(STREAM_POSITIONS, QUERY_HEADS, HEAD_SIZE).transpose(1, 0, 2)
        o_heads = output.reshape(STREAM_POSITIONS, QUERY_HEADS, HEAD_SIZE).transpose(1, 0, 2)
        key_head_rows = key.reshape(STREAM_POSITIONS, KEY_VALUE_HEADS, HEAD_SIZE).transpose(1, 0, 2)
        value_head_rows = value_rows.reshape(STREAM_POSITIONS, KEY_VALUE_HEADS, HEAD_SIZE).transpose(1, 0, 2)

        def one_head(head_items):
            q_one, u_one, o_one, index = head_items
            kv_index = (index // query_group_size).astype(jnp.int32)
            k_one = lax.dynamic_index_in_dim(key_head_rows, kv_index, 0, keepdims=False)
            v_one = lax.dynamic_index_in_dim(value_head_rows, kv_index, 0, keepdims=False)
            return head_grads(q_one, u_one, o_one, k_one, v_one, segments)

        dquery, key_gradient, value_gradient = lax.map(one_head, (q_heads, u_heads, o_heads, jnp.arange(QUERY_HEADS, dtype=jnp.int32)))
        dquery = dquery.transpose(1, 0, 2).reshape(STREAM_POSITIONS, QUERY_HEADS * HEAD_SIZE)
        key_gradient = partial_sum(key_gradient, query_group_size, per_tenant_slot)
        value_gradient = partial_sum(value_gradient, query_group_size, per_tenant_slot)
        key_gradient = key_gradient.transpose(1, 0, 2).reshape(STREAM_POSITIONS, KEY_VALUE_HEADS * HEAD_SIZE)
        value_gradient = value_gradient.transpose(1, 0, 2).reshape(STREAM_POSITIONS, KEY_VALUE_HEADS * HEAD_SIZE)
        return dquery, key_gradient, value_gradient

    queries_gradient, keys_gradient, values_gradient = lax.map(one_group, (queries, keys, values, outputs, upstream, lengths))

    def owner_rows(items):
        lens, tens = items
        segments = segment_ids(lens, jnp.arange(STREAM_POSITIONS, dtype=jnp.int32))
        return tenant_ids(segments, tens)

    owners = lax.map(owner_rows, (lengths, tenants)).reshape(STREAM_COUNT * STREAM_POSITIONS)
    column_indices = (jnp.arange(TENANT_COUNT * ADAPTER_RANK, dtype=jnp.int32) // ADAPTER_RANK).astype(jnp.int32)
    owned = column_indices[None, :] == owners[:, None]
    flattened_inputs = inputs.reshape(STREAM_COUNT * STREAM_POSITIONS, MODEL_WIDTH)
    flattened_values = values_gradient.reshape(STREAM_COUNT * STREAM_POSITIONS, KEY_VALUE_HEADS * HEAD_SIZE)
    low_rank_state = jnp.dot(flattened_inputs, adapter_down_maps, preferred_element_type=jnp.float32)
    low_rank_state = jnp.where(owned, low_rank_state, 0.0).astype(jnp.bfloat16)
    backward_pass = jnp.dot(flattened_values, adapter_up_maps.T, preferred_element_type=jnp.float32) * adapter_scale
    backward_pass = jnp.where(owned, backward_pass, 0.0).astype(jnp.bfloat16)
    down_map_gradient = jnp.dot(flattened_inputs.T, backward_pass, preferred_element_type=jnp.float32)
    up_map_gradient = jnp.dot(low_rank_state.T, flattened_values, preferred_element_type=jnp.float32) * adapter_scale
    return queries_gradient, keys_gradient, values_gradient, down_map_gradient, up_map_gradient
```

```python
import functools
import math

import jax
import jax.numpy as jnp
from jax import lax
from jax.experimental import pallas as pl
from jax.experimental.pallas import tpu as pltpu
from jax.sharding import PartitionSpec as P

HEAD_SIZE = 128
ADAPTER_RANK = 16
TENANTS = 8
DOCS = 8
SLOTS = 16
TOK = 128
BACK = 8
CHUNKS = BACK + 1
PAIRS = 16
SCALE = HEAD_SIZE**-0.5
LOG2E_SCALE = SCALE * math.log2(math.e)
NEG = -1e30
F32 = jnp.float32
BF16 = jnp.bfloat16
VMEM_LIMIT = 40 * 1024 * 1024

adapter_scale = 2.0


def dot_nt(a, b):
    return lax.dot_general(a, b, (((1,), (1,)), ((), ())), preferred_element_type=F32)


def dot(a, b):
    return jnp.dot(a, b, preferred_element_type=F32)


def doc_rows(len_ref, ten_ref, pos):
    begin = jnp.int32(0)
    start = jnp.zeros_like(pos)
    tenant = jnp.zeros_like(pos)
    for d in range(DOCS):
        inside = pos >= begin
        start = jnp.where(inside, begin, start)
        tenant = jnp.where(inside, ten_ref[0, d], tenant)
        begin = begin + len_ref[0, d]
    return start, tenant


def chunk_positions(chunk):
    return chunk * TOK + lax.broadcasted_iota(jnp.int32, (1, TOK), 1)


def fold(full, tenant):
    out = jnp.zeros((ADAPTER_RANK, TOK), F32)
    for t in range(TENANTS):
        out = out + jnp.where(tenant == t, full[t * ADAPTER_RANK : (t + 1) * ADAPTER_RANK], 0.0)
    return out


def expand(rows, tenant):
    return jnp.concatenate([jnp.where(tenant == t, rows, 0.0) for t in range(TENANTS)], axis=0)


def fill_bias(len_ref, ten_ref, me, bias):
    query = chunk_positions(me)
    start, _ = doc_rows(len_ref, ten_ref, query)
    for c in range(CHUNKS):
        key = (me - c) * TOK + lax.broadcasted_iota(jnp.int32, (TOK, TOK), 0)
        bias[c] = jnp.where((key >= start) & (key <= query), 0.0, NEG)


def pair_rows(ref, p):
    at = pl.multiple_of(p * 256, 256)
    return jnp.concatenate([ref[:, pl.ds(at, 128)], ref[:, pl.ds(at + 128, 128)]], axis=0)


def prep_kernel(len_ref, ten_ref, x_ref, d_ref, u_ref, o_ref, low_ref, delta_ref):
    me = lax.axis_index("seq")
    low = dot(x_ref[...], d_ref[...])
    _, tenant = doc_rows(len_ref, ten_ref, chunk_positions(me))
    low_ref[...] = fold(low.T, tenant).astype(BF16)
    for h in range(2 * PAIRS):
        lanes = slice(h * 128, (h + 1) * 128)
        product = u_ref[:, lanes].astype(F32) * o_ref[:, lanes].astype(F32)
        row = jnp.sum(product.T, axis=0, keepdims=True)
        delta_ref[h // 2 : h // 2 + 1, (h % 2) * 128 : (h % 2 + 1) * 128] = row


def values_kernel(len_ref, ten_ref, q_ref, u_ref, low_ref, up_ref, *refs):
    k_refs, refs = refs[:CHUNKS], refs[CHUNKS:]
    dv_refs, refs = refs[:CHUNKS], refs[CHUNKS:]
    slots_ref, upart_ref, m_ref, rl_ref, bias, weights, acc = refs
    me = lax.axis_index("seq")
    fill_bias(len_ref, ten_ref, me, bias)
    acc[...] = jnp.zeros_like(acc)

    def pair(p, carry):
        queries, upstream = pair_rows(q_ref, p), pair_rows(u_ref, p)
        lanes = pl.ds(pl.multiple_of((p // 4) * 128, 128), 128)
        top = jnp.full((8, 256), NEG, F32)
        for c in range(CHUNKS):
            s = dot_nt(k_refs[c][:, lanes], queries)
            b = bias[c]
            s = s + jnp.concatenate([b, b], axis=1)
            weights[c] = s
            top = jnp.maximum(top, jnp.max(s.reshape(16, 8, 256), axis=0))
        top = jnp.max(top, axis=0, keepdims=True)
        total = jnp.zeros((8, 256), F32)
        for c in range(CHUNKS):
            e = jnp.exp2((weights[c] - top) * LOG2E_SCALE)
            weights[c] = e
            total = total + jnp.sum(e.reshape(16, 8, 256), axis=0)
        inverse = 1.0 / jnp.sum(total, axis=0, keepdims=True)
        for c in range(CHUNKS):
            prob = (weights[c] * inverse).astype(BF16)
            acc[c, :, lanes] += dot(prob, upstream)
        m_ref[pl.ds(p, 1), :] = top
        rl_ref[pl.ds(p, 1), :] = inverse
        return carry

    lax.fori_loop(0, PAIRS, pair, 0)
    slots_ref[...] = jnp.zeros_like(slots_ref)
    upart = jnp.zeros(upart_ref.shape, F32)
    for c in range(CHUNKS):
        dv = acc[c].astype(BF16)
        dv_refs[c][...] = dv
        _, tenant = doc_rows(len_ref, ten_ref, chunk_positions(me - c))
        owner = lax.rem(me - c + SLOTS, SLOTS)
        back = dot_nt(up_ref[...], dv) * adapter_scale
        slots_ref[owner] = fold(back, tenant).astype(BF16)
        low = expand(low_ref[owner].astype(F32), tenant).astype(BF16)
        upart = upart + dot(low, dv)
    upart_ref[...] = upart * adapter_scale


def keys_kernel(len_ref, ten_ref, q_ref, u_ref, m_ref, rl_ref, delta_ref, *refs):
    k_refs, refs = refs[:CHUNKS], refs[CHUNKS:]
    v_refs, refs = refs[:CHUNKS], refs[CHUNKS:]
    dq_ref, refs = refs[0], refs[1:]
    dk_refs, refs = refs[:CHUNKS], refs[CHUNKS:]
    bias, dscores, key_t, acc = refs
    me = lax.axis_index("seq")
    fill_bias(len_ref, ten_ref, me, bias)
    acc[...] = jnp.zeros_like(acc)
    for kv in range(4):
        for c in range(CHUNKS):
            key_t[kv, :, c * 128 : (c + 1) * 128] = (
                k_refs[c][:, kv * 128 : (kv + 1) * 128].astype(F32).T.astype(BF16)
            )

    def pair(p, carry):
        queries, upstream = pair_rows(q_ref, p), pair_rows(u_ref, p)
        kv = p // 4
        lanes = pl.ds(pl.multiple_of(kv * 128, 128), 128)
        top = m_ref[pl.ds(p, 1), :]
        inverse = rl_ref[pl.ds(p, 1), :]
        delta = delta_ref[pl.ds(p, 1), :]
        for c in range(CHUNKS):
            b = bias[c]
            s = dot_nt(k_refs[c][:, lanes], queries) + jnp.concatenate([b, b], axis=1)
            prob = jnp.exp2((s - top) * LOG2E_SCALE) * inverse
            dprob = dot_nt(v_refs[c][:, lanes], upstream)
            dscore = (prob * (dprob - delta)).astype(BF16)
            dscores[c * 128 : (c + 1) * 128, :] = dscore
            acc[c, :, lanes] += dot(dscore, queries)
        dq = (dot(key_t[kv], dscores[...]) * SCALE).T.astype(BF16)
        at = pl.multiple_of(p * 256, 256)
        dq_ref[:, pl.ds(at, 128)] = dq[:128]
        dq_ref[:, pl.ds(at + 128, 128)] = dq[128:]
        return carry

    lax.fori_loop(0, PAIRS, pair, 0)
    for c in range(CHUNKS):
        dk_refs[c][...] = (acc[c] * SCALE).astype(BF16)


def maps_kernel(len_ref, ten_ref, x_ref, slots_ref, upart_ref, keep_ref, send_ref):
    me = lax.axis_index("seq")
    core = lax.rem(lax.axis_index("grp"), 2)
    _, tenant = doc_rows(len_ref, ten_ref, chunk_positions(me))
    rows = jnp.zeros((ADAPTER_RANK, TOK), F32)
    for j in range(SLOTS):
        rows = rows + slots_ref[j].astype(F32)
    back = expand(rows, tenant).astype(BF16)
    half = keep_ref.shape[1]
    width = x_ref.shape[1]

    def halves(first, second):
        first[...] = dot(back, x_ref[:, :half]).astype(BF16)
        second[:, : width - half] = dot(back, x_ref[:, half:]).astype(BF16)
        second[:, width - half :] = upart_ref[...].astype(BF16)

    pl.when(core == 0)(lambda: halves(keep_ref, send_ref))
    pl.when(core == 1)(lambda: halves(send_ref, keep_ref))


def final_kernel(mine_ref, other_ref, down_ref, up_ref):
    core = lax.rem(lax.axis_index("grp"), 2)
    half = mine_ref.shape[1]
    width = down_ref.shape[0]

    def write(first, second):
        for at in range(0, width, 128):
            ref, base = (first, at) if at < half else (second, at - half)
            down_ref[at : at + 128, :] = ref[:, base : base + 128].astype(F32).T
        up_ref[...] = second[:, width - half :].astype(F32)

    pl.when(core == 0)(lambda: write(mine_ref, other_ref))
    pl.when(core == 1)(lambda: write(other_ref, mine_ref))


def call(kernel, out_shape, n_in, scratch=()):
    smem = pl.BlockSpec(memory_space=pltpu.SMEM)
    vmem = pl.BlockSpec(memory_space=pltpu.VMEM)
    n_smem = 0 if kernel is final_kernel else 2
    return pl.pallas_call(
        kernel,
        out_shape=out_shape,
        in_specs=[smem] * n_smem + [vmem] * n_in,
        out_specs=jax.tree.map(lambda _: vmem, out_shape),
        scratch_shapes=list(scratch),
        compiler_params=pltpu.CompilerParams(vmem_limit_bytes=VMEM_LIMIT),
    )


def shape(dims, dtype):
    return jax.ShapeDtypeStruct(dims, dtype)


def shifted(array, by):
    return lax.ppermute(array, "seq", [(i, (i + by) % SLOTS) for i in range(SLOTS)])


def swap(array, distance):
    count = lax.axis_size("grp")
    return lax.ppermute(array, "grp", [(i, i ^ distance) for i in range(count)])


def spread(array):
    return lax.all_to_all(array, "seq", split_axis=0, concat_axis=0, tiled=True)


def after(array, *others):
    return lax.optimization_barrier((array,) + others)[0]


def per_device(
    inputs,
    queries,
    keys,
    values,
    outputs,
    upstream,
    lengths,
    tenants,
    adapter_down_maps,
    adapter_up_maps,
):
    x, q, k, v, o, u = (a[0] for a in (inputs, queries, keys, values, outputs, upstream))
    width, kv_width = x.shape[1], k.shape[1]
    half = (width + kv_width) // 2
    ranks = TENANTS * ADAPTER_RANK

    k_chunks = [k] + [shifted(k, s) for s in range(1, CHUNKS)]
    low, delta = call(
        prep_kernel,
        (shape((ADAPTER_RANK, TOK), BF16), shape((PAIRS, 256), F32)),
        4,
    )(lengths, tenants, x, adapter_down_maps, u, o)
    low_all = spread(jnp.broadcast_to(low[None], (SLOTS, ADAPTER_RANK, TOK)))

    part = shape((TOK, kv_width), BF16)
    bias = pltpu.VMEM((CHUNKS, TOK, TOK), F32)
    acc = pltpu.VMEM((CHUNKS, TOK, kv_width), F32)
    *dv_parts, slots, upart, top, inverse = call(
        values_kernel,
        (part,) * CHUNKS
        + (
            shape((SLOTS, ADAPTER_RANK, TOK), BF16),
            shape((ranks, kv_width), F32),
            shape((PAIRS, 256), F32),
            shape((PAIRS, 256), F32),
        ),
        4 + CHUNKS,
        (bias, pltpu.VMEM((CHUNKS, TOK, 256), F32), acc),
    )(lengths, tenants, q, u, low_all, adapter_up_maps, *k_chunks)

    v_late = after(v, *k_chunks)
    v_chunks = [v] + [shifted(v_late, s) for s in range(1, CHUNKS)]

    slots = spread(slots)
    keep, send = call(
        maps_kernel,
        (shape((ranks, half), BF16), shape((ranks, half), BF16)),
        3,
    )(lengths, tenants, x, slots, upart)
    got = swap(send, 1)
    mixed = (keep.astype(F32) + got.astype(F32)).astype(BF16)
    mixed = spread(mixed.reshape(SLOTS, ranks // SLOTS, half))

    dq, *dk_parts = call(
        keys_kernel,
        (shape(q.shape, BF16),) + (part,) * CHUNKS,
        5 + 2 * CHUNKS,
        (
            bias,
            pltpu.VMEM((CHUNKS * TOK, 256), BF16),
            pltpu.VMEM((kv_width // 128, 128, CHUNKS * TOK), BF16),
            acc,
        ),
    )(lengths, tenants, q, u, top, inverse, delta, *k_chunks, *v_chunks)

    dv_home = [dv_parts[0]] + [shifted(dv_parts[s], -s) for s in range(1, CHUNKS)]
    dk_home = [dk_parts[0]] + [shifted(dk_parts[s], -s) for s in range(1, CHUNKS)]
    values_gradient = functools.reduce(jnp.add, [a.astype(F32) for a in dv_home]).astype(BF16)
    keys_gradient = functools.reduce(jnp.add, [a.astype(F32) for a in dk_home]).astype(BF16)

    total = jnp.sum(mixed.astype(F32), axis=0)
    distance = 2
    while distance < lax.axis_size("grp"):
        short = lax.optimization_barrier(total.astype(BF16))
        total = short.astype(F32) + swap(short, distance).astype(F32)
        distance *= 2
    total = lax.optimization_barrier(total.astype(BF16))
    mine = spread(jnp.broadcast_to(total[None], (SLOTS, ranks // SLOTS, half)))
    mine = mine.reshape(ranks, half)
    other = swap(mine, 1)
    down, up = call(
        final_kernel,
        (shape((width, ranks), F32), shape((ranks, kv_width), F32)),
        2,
    )(mine, other)
    return dq[None], keys_gradient[None], values_gradient[None], down, up


def solution(mesh):
    in_specs = (
        P("grp", "seq", None),
        P("grp", "seq", None),
        P("grp", "seq", None),
        P("grp", "seq", None),
        P("grp", "seq", None),
        P("grp", "seq", None),
        P("grp", None),
        P("grp", None),
        P(),
        P(),
    )
    out_specs = (P("grp", "seq", None), P("grp", "seq", None), P("grp", "seq", None), P(), P())
    return jax.shard_map(
        per_device, mesh=mesh, in_specs=in_specs, out_specs=out_specs, check_vma=False
    )
```

```python
import functools
import math

import jax
import jax.numpy as jnp
from jax import lax
from jax.experimental import pallas as pl
from jax.experimental.pallas import tpu as pltpu
from jax.sharding import PartitionSpec as P

HEAD_SIZE = 128
ADAPTER_RANK = 16
TENANTS = 8
DOCS = 8
SLOTS = 16
TOK = 128
BACK = 8
CHUNKS = BACK + 1
KV_HEADS = 4
GROUP = 8
SCALE = HEAD_SIZE**-0.5
LOG2E_SCALE = SCALE * math.log2(math.e)
NEG = -1e30
F32 = jnp.float32
BF16 = jnp.bfloat16
VMEM_LIMIT = 60 * 1024 * 1024

adapter_scale = 2.0


def dot_nt(a, b):
    return lax.dot_general(a, b, (((1,), (1,)), ((), ())), preferred_element_type=F32)


def dot(a, b):
    return jnp.dot(a, b, preferred_element_type=F32)


def doc_rows(len_ref, ten_ref, pos):
    begin = jnp.int32(0)
    start = jnp.zeros_like(pos)
    tenant = jnp.zeros_like(pos)
    for d in range(DOCS):
        inside = pos >= begin
        start = jnp.where(inside, begin, start)
        tenant = jnp.where(inside, ten_ref[0, d], tenant)
        begin = begin + len_ref[0, d]
    return start, tenant


def chunk_positions(chunk):
    return chunk * TOK + lax.broadcasted_iota(jnp.int32, (1, TOK), 1)


def fold(full, tenant):
    out = jnp.zeros((ADAPTER_RANK, TOK), F32)
    for t in range(TENANTS):
        out = out + jnp.where(tenant == t, full[t * ADAPTER_RANK : (t + 1) * ADAPTER_RANK], 0.0)
    return out


def expand(rows, tenant):
    return jnp.concatenate([jnp.where(tenant == t, rows, 0.0) for t in range(TENANTS)], axis=0)


def fill_bias(len_ref, ten_ref, me, bias):
    query = chunk_positions(me)
    start, _ = doc_rows(len_ref, ten_ref, query)
    for c in range(CHUNKS):
        key = (me - c) * TOK + lax.broadcasted_iota(jnp.int32, (TOK, TOK), 0)
        bias[c] = jnp.where((key >= start) & (key <= query), 0.0, NEG)


def stacked(ref, kv):
    at = kv * GROUP
    return jnp.concatenate(
        [ref[:, (at + h) * HEAD_SIZE : (at + h + 1) * HEAD_SIZE] for h in range(GROUP)], axis=0
    )


def copies(sems, pairs):
    started = [pltpu.make_async_copy(a, b, sems.at[i]) for i, (a, b) in enumerate(pairs)]
    for one in started:
        one.start()
    return started


def wait(started):
    for one in started:
        one.wait()


def rows(c):
    return pl.ds(c * TOK, TOK)


def prep_kernel(len_ref, ten_ref, x_ref, d_ref, u_ref, o_ref, low_ref, delta_ref):
    me = lax.axis_index("seq")
    low = dot(x_ref[...], d_ref[...])
    _, tenant = doc_rows(len_ref, ten_ref, chunk_positions(me))
    low_ref[...] = fold(low.T, tenant).astype(BF16)
    for h in range(delta_ref.shape[1] // TOK):
        lanes = slice(h * 128, (h + 1) * 128)
        product = u_ref[:, lanes].astype(F32) * o_ref[:, lanes].astype(F32)
        delta_ref[:, lanes] = jnp.sum(product.T, axis=0, keepdims=True)


def biased(bias, c, weights, at):
    b = bias[c]
    return weights[rows(c), at : at + 256] + jnp.concatenate([b, b], axis=1)


def blocks(parts, whole):
    out, first = [], 0
    for part in parts:
        out.append((part.at[:, pl.ds(0, whole.shape[1])], whole.at[pl.ds(first, part.shape[0])]))
        first += part.shape[0]
    return out


def values_kernel(len_ref, ten_ref, up_ref, low_ref, q_hbm, u_hbm, *refs):
    k_hbm, refs = refs[:CHUNKS], refs[CHUNKS:]
    dv_hbm, odd_hbm, high_hbm, low_hbm, last_hbm, slots_ref, top_ref, inverse_ref, *refs = refs
    q_ref, u_ref, k_ref, dv_ref, bias, weights, probs, sems = refs
    started = copies(sems, [(q_hbm, q_ref), (u_hbm, u_ref)] + blocks(k_hbm, k_ref))
    me = lax.axis_index("seq")
    fill_bias(len_ref, ten_ref, me, bias)
    wait(started)
    for kv in range(KV_HEADS):
        lanes = slice(kv * HEAD_SIZE, (kv + 1) * HEAD_SIZE)
        weights[...] = dot_nt(k_ref[:, lanes], stacked(q_ref, kv))
        for at in range(0, GROUP * TOK, 256):
            top = jnp.full((8, 256), NEG, F32)
            for c in range(CHUNKS):
                s = biased(bias, c, weights, at)
                weights[rows(c), at : at + 256] = s
                top = jnp.maximum(top, jnp.max(s.reshape(16, 8, 256), axis=0))
            top = jnp.max(top, axis=0, keepdims=True)
            total = jnp.zeros((8, 256), F32)
            for c in range(CHUNKS):
                e = jnp.exp2((weights[rows(c), at : at + 256] - top) * LOG2E_SCALE)
                weights[rows(c), at : at + 256] = e
                total = total + jnp.sum(e.reshape(16, 8, 256), axis=0)
            inverse = 1.0 / jnp.sum(total, axis=0, keepdims=True)
            for c in range(CHUNKS):
                probs[rows(c), at : at + 256] = (
                    weights[rows(c), at : at + 256] * inverse
                ).astype(BF16)
            wide = kv * GROUP * TOK + at
            top_ref[:, wide : wide + 256] = top
            inverse_ref[:, wide : wide + 256] = inverse
        dv_ref[:, lanes] = dot(probs[...], stacked(u_ref, kv)).astype(BF16)
    homes = [(odd_hbm, (1, 3, 5, 7)), (high_hbm, (4, 6)), (low_hbm, (0, 2)), (last_hbm, (8,))]
    out = copies(
        sems,
        [(dv_ref, dv_hbm)]
        + [(dv_ref.at[rows(c)], home.at[rows(n)]) for home, cs in homes for n, c in enumerate(cs)],
    )
    for j in range(SLOTS):
        slots_ref[j, :ADAPTER_RANK] = jnp.zeros((ADAPTER_RANK, TOK), BF16)
        slots_ref[j, ADAPTER_RANK:] = low_ref[...]
    for c in range(CHUNKS):
        _, tenant = doc_rows(len_ref, ten_ref, chunk_positions(me - c))
        back = dot_nt(up_ref[...], dv_ref[rows(c), :]) * adapter_scale
        owner = lax.rem(me - c + SLOTS, SLOTS)
        slots_ref[owner, :ADAPTER_RANK] = fold(back, tenant).astype(BF16)
    wait(out)


def keys_kernel(len_ref, ten_ref, top_ref, inverse_ref, delta_ref, q_hbm, u_hbm, dv_hbm, *refs):
    k_hbm, refs = refs[:CHUNKS], refs[CHUNKS:]
    v_hbm, refs = refs[:3], refs[3:]
    dq_hbm, *dk_hbm, last_hbm, q_ref, u_ref, k_ref, v_ref, dq_ref, dk_ref, dv_ref = refs[:13]
    bias, weights, dprobs, dscores, sems = refs[13:]
    kv_width = k_ref.shape[1]
    me = lax.axis_index("seq")
    started = copies(
        sems,
        [(q_hbm, q_ref), (u_hbm, u_ref), (dv_hbm, dv_ref)]
        + blocks(k_hbm, k_ref)
        + blocks(v_hbm, v_ref),
    )
    fill_bias(len_ref, ten_ref, me, bias)
    wait(started)
    for kv in range(KV_HEADS):
        lanes = slice(kv * HEAD_SIZE, (kv + 1) * HEAD_SIZE)
        queries, upstream = stacked(q_ref, kv), stacked(u_ref, kv)
        weights[...] = dot_nt(k_ref[:, lanes], queries)
        dprobs[...] = dot_nt(v_ref[:, lanes], upstream)
        for at in range(0, GROUP * TOK, 256):
            wide = kv * GROUP * TOK + at
            top = top_ref[:, wide : wide + 256]
            inverse = inverse_ref[:, wide : wide + 256]
            delta = delta_ref[:, wide : wide + 256]
            for c in range(CHUNKS):
                s = biased(bias, c, weights, at)
                prob = jnp.exp2((s - top) * LOG2E_SCALE) * inverse
                dprob = dprobs[rows(c), at : at + 256]
                dscores[rows(c), at : at + 256] = (prob * (dprob - delta)).astype(BF16)
        dk_ref[:, lanes] = (dot(dscores[...], queries) * SCALE).astype(BF16)
        key_t = k_ref[:, lanes].astype(F32).T.astype(BF16)
        dq = dot(key_t, dscores[...]) * SCALE
        for h in range(GROUP):
            at = (kv * GROUP + h) * HEAD_SIZE
            dq_ref[:, at : at + HEAD_SIZE] = dq[:, h * TOK : (h + 1) * TOK].T.astype(BF16)
    out = [
        (dq_ref, dq_hbm),
        (dk_ref.at[rows(8)], last_hbm.at[:, pl.ds(0, kv_width)]),
        (dv_ref, last_hbm.at[:, pl.ds(kv_width, kv_width)]),
    ]
    out += [(b, a) for a, b in blocks(dk_hbm, dk_ref)]
    wait(copies(sems, out))


def maps_kernel(len_ref, ten_ref, slots_ref, dv_hbm, x_hbm, keep_ref, send_ref, x_ref, dv_ref, sems):
    started = copies(sems, [(x_hbm, x_ref), (dv_hbm, dv_ref)])
    me = lax.axis_index("seq")
    core = lax.rem(lax.axis_index("grp"), 2)
    total = jnp.zeros((ADAPTER_RANK, TOK), F32)
    for j in range(SLOTS):
        total = total + slots_ref[j, :ADAPTER_RANK].astype(F32)
    low = []
    for c in range(CHUNKS):
        owner = lax.rem(me - c + SLOTS, SLOTS)
        _, tenant = doc_rows(len_ref, ten_ref, chunk_positions(me - c))
        low.append(expand(slots_ref[owner, ADAPTER_RANK:].astype(F32), tenant).astype(BF16))
    _, tenant = doc_rows(len_ref, ten_ref, chunk_positions(me))
    back = expand(total, tenant).astype(BF16)
    half = keep_ref.shape[1]
    width = x_ref.shape[1]
    wait(started)
    upart = (dot(jnp.concatenate(low, axis=1), dv_ref[...]) * adapter_scale).astype(BF16)

    def halves(first, second):
        first[...] = dot(back, x_ref[:, :half]).astype(BF16)
        second[:, : width - half] = dot(back, x_ref[:, half:]).astype(BF16)
        second[:, width - half :] = upart

    pl.when(core == 0)(lambda: halves(keep_ref, send_ref))
    pl.when(core == 1)(lambda: halves(send_ref, keep_ref))


def final_kernel(mine_ref, other_ref, down_ref, up_ref):
    core = lax.rem(lax.axis_index("grp"), 2)
    half = mine_ref.shape[1]
    width = down_ref.shape[0]

    def write(first, second):
        for at in range(0, width, 128):
            ref, base = (first, at) if at < half else (second, at - half)
            down_ref[at : at + 128, :] = ref[:, base : base + 128].astype(F32).T
        up_ref[...] = second[:, width - half :].astype(F32)

    pl.when(core == 0)(lambda: write(mine_ref, other_ref))
    pl.when(core == 1)(lambda: write(other_ref, mine_ref))


S, V, H = pltpu.SMEM, pltpu.VMEM, pltpu.HBM


def call(kernel, ins, outs, scratch=(), products=0, exps=0, moved=0):
    return pl.pallas_call(
        kernel,
        out_shape=tuple(jax.ShapeDtypeStruct(dims, dtype) for _, dims, dtype in outs),
        in_specs=[pl.BlockSpec(memory_space=m) for m in ins],
        out_specs=tuple(pl.BlockSpec(memory_space=m) for m, _, _ in outs),
        scratch_shapes=list(scratch),
        compiler_params=pltpu.CompilerParams(vmem_limit_bytes=VMEM_LIMIT),
        cost_estimate=pl.CostEstimate(flops=2 * products, transcendentals=exps, bytes_accessed=moved),
    )


def shifted(array, by):
    return lax.ppermute(array, "seq", [(i, (i + by) % SLOTS) for i in range(SLOTS)])


def swap(array, distance):
    count = lax.axis_size("grp")
    return lax.ppermute(array, "grp", [(i, i ^ distance) for i in range(count)])


def spread(array):
    return lax.all_to_all(array, "seq", split_axis=0, concat_axis=0, tiled=True)


def add(*arrays):
    return functools.reduce(jnp.add, [a.astype(F32) for a in arrays])


def after(array, *others):
    return lax.optimization_barrier((array,) + others)[0]


def per_device(
    inputs,
    queries,
    keys,
    values,
    outputs,
    upstream,
    lengths,
    tenants,
    adapter_down_maps,
    adapter_up_maps,
):
    x, q, k, v, o, u = (a[0] for a in (inputs, queries, keys, values, outputs, upstream))
    width, kv_width, q_width = x.shape[1], k.shape[1], q.shape[1]
    half = (width + kv_width) // 2
    ranks = TENANTS * ADAPTER_RANK
    tables = (lengths, tenants)
    work = CHUNKS * TOK * q_width
    row = (V, (1, q_width), F32)
    span = (CHUNKS * TOK, GROUP * TOK)
    bias = V((CHUNKS, TOK, TOK), F32)

    def array(chunks, lanes=kv_width):
        return (H, (chunks * TOK, lanes), BF16)

    low, delta = call(
        prep_kernel,
        [S, S] + [V] * 4,
        [(V, (ADAPTER_RANK, TOK), BF16), row],
        products=16 * work * HEAD_SIZE,
        moved=8 * work,
    )(*tables, x, adapter_down_maps, u, o)
    kv_1 = shifted(jnp.concatenate([k, v], axis=1), 1)
    k_chunks = [k, kv_1] + [shifted(k, s) for s in range(2, CHUNKS)]
    v_home = v
    v_8 = shifted(v_home, 8)
    v_01 = jnp.concatenate([v_home, kv_1[:, kv_width:]], axis=0)
    v_23 = shifted(v_01, 2)

    dv_parts, odd, high, even, dv_last, slots, top, inverse = call(
        values_kernel,
        [S, S, V, V, H, H] + [H] * CHUNKS,
        [
            array(CHUNKS),
            array(4),
            array(2),
            array(2),
            array(1),
            (V, (SLOTS, 2 * ADAPTER_RANK, TOK), BF16),
            row,
            row,
        ],
        [
            V(q.shape, BF16),
            V(u.shape, BF16),
            V((CHUNKS * TOK, kv_width), BF16),
            V((CHUNKS * TOK, kv_width), BF16),
            bias,
            V(span, F32),
            V(span, BF16),
            pltpu.SemaphoreType.DMA((2 + CHUNKS,)),
        ],
        32 * work * HEAD_SIZE,
        work,
        12 * work,
    )(*tables, adapter_up_maps, low, q, u, *k_chunks)
    v_0123 = after(jnp.concatenate([v_01, v_23], axis=0), slots)
    v_4567 = shifted(v_0123, 4)
    slots = spread(after(slots, v_23))
    keep, send = call(
        maps_kernel,
        [S, S, V, H, H],
        [(V, (ranks, half), BF16)] * 2,
        [
            V(x.shape, BF16),
            V((CHUNKS * TOK, kv_width), BF16),
            pltpu.SemaphoreType.DMA((2,)),
        ],
    )(*tables, after(slots, v_4567, v_8), dv_parts, x)
    odd = shifted(odd, -1)
    got = swap(send, 1)
    mixed = (keep.astype(F32) + got.astype(F32)).astype(BF16)
    mixed = after(mixed.reshape(SLOTS, ranks // SLOTS, half), v_4567, v_8)
    mixed = spread(mixed)
    total = jnp.sum(mixed.astype(F32), axis=0)

    dq, near, middle, far, farthest, last = call(
        keys_kernel,
        [S, S, V, V, V, H, H, H] + [H] * (CHUNKS + 3),
        [(H, q.shape, BF16), *map(array, (2, 2, 2, 2)), array(1, 2 * kv_width)],
        [
            V(q.shape, BF16),
            V(u.shape, BF16),
            V((CHUNKS * TOK, kv_width), BF16),
            V((CHUNKS * TOK, kv_width), BF16),
            V(q.shape, BF16),
            V((CHUNKS * TOK, kv_width), BF16),
            V(v.shape, BF16),
            bias,
            V(span, F32),
            V(span, F32),
            V(span, BF16),
            pltpu.SemaphoreType.DMA((3 + CHUNKS + 3,)),
        ],
        32 * work * HEAD_SIZE,
        work,
        12 * work,
    )(*tables, top, inverse, delta, q, u, dv_last, *k_chunks, v_0123, v_4567, v_8)
    farthest, far, last = shifted(farthest, -4), shifted(far, -4), shifted(last, -8)

    two = 2 * TOK
    middle = shifted(add(middle, farthest).astype(BF16), -2)
    high = shifted(add(high, odd[two:]).astype(BF16), -4)
    near = add(near, far, middle)
    even = add(even, odd[:two], high)
    near_out = shifted(near[TOK:].astype(BF16), -1)
    even_out = shifted(even[TOK:].astype(BF16), -2)
    keys_gradient = add(near[:TOK], near_out, last[:, :kv_width]).astype(BF16)
    values_gradient = add(even[:TOK], even_out, last[:, kv_width:]).astype(BF16)

    beside = {2: (dq, odd), 8: (farthest, high)}
    distance = 2
    while distance < lax.axis_size("grp"):
        short = after(total.astype(BF16), *beside.get(distance, ()))
        total = short.astype(F32) + swap(short, distance).astype(F32)
        distance *= 2
    total = after(total.astype(BF16), far, middle)
    mine = spread(jnp.broadcast_to(total[None], (SLOTS, ranks // SLOTS, half)))
    mine = mine.reshape(ranks, half)
    other = swap(after(mine, near_out, even_out, last), 1)
    down, up = call(
        final_kernel, [V, V], [(V, (width, ranks), F32), (V, (ranks, kv_width), F32)]
    )(mine, other)
    return dq[None], keys_gradient[None], values_gradient[None], down, up


def solution(mesh):
    in_specs = (
        P("grp", "seq", None),
        P("grp", "seq", None),
        P("grp", "seq", None),
        P("grp", "seq", None),
        P("grp", "seq", None),
        P("grp", "seq", None),
        P("grp", None),
        P("grp", None),
        P(),
        P(),
    )
    out_specs = (P("grp", "seq", None), P("grp", "seq", None), P("grp", "seq", None), P(), P())
    return jax.shard_map(
        per_device, mesh=mesh, in_specs=in_specs, out_specs=out_specs, check_vma=False
    )
```

```python
import functools
import math

import jax
import jax.numpy as jnp
from jax import lax
from jax.experimental import pallas as pl
from jax.experimental.pallas import tpu as pltpu
from jax.sharding import PartitionSpec as P

HEAD_SIZE = 128
ADAPTER_RANK = 16
TENANTS = 8
DOCS = 8
SLOTS = 16
TOK = 128
BACK = 8
CHUNKS = BACK + 1
KV_HEADS = 4
GROUP = 8
SCALE = HEAD_SIZE**-0.5
LOG2E_SCALE = SCALE * math.log2(math.e)
NEG = -1e30
F32 = jnp.float32
BF16 = jnp.bfloat16
VMEM_LIMIT = 60 * 1024 * 1024

adapter_scale = 2.0


def dot_nt(a, b):
    return lax.dot_general(a, b, (((1,), (1,)), ((), ())), preferred_element_type=F32)


def dot(a, b):
    return jnp.dot(a, b, preferred_element_type=F32)


def doc_rows(len_ref, ten_ref, pos):
    begin = jnp.int32(0)
    start = jnp.zeros_like(pos)
    tenant = jnp.zeros_like(pos)
    for d in range(DOCS):
        inside = pos >= begin
        start = jnp.where(inside, begin, start)
        tenant = jnp.where(inside, ten_ref[0, d], tenant)
        begin = begin + len_ref[0, d]
    return start, tenant


def chunk_positions(chunk):
    return chunk * TOK + lax.broadcasted_iota(jnp.int32, (1, TOK), 1)


def fold(full, tenant):
    out = jnp.zeros((ADAPTER_RANK, TOK), F32)
    for t in range(TENANTS):
        out = out + jnp.where(tenant == t, full[t * ADAPTER_RANK : (t + 1) * ADAPTER_RANK], 0.0)
    return out


def expand(rows, tenant):
    return jnp.concatenate([jnp.where(tenant == t, rows, 0.0) for t in range(TENANTS)], axis=0)


def fill_bias(len_ref, ten_ref, me, bias):
    query = chunk_positions(me)
    start, _ = doc_rows(len_ref, ten_ref, query)
    for c in range(CHUNKS):
        key = (me - c) * TOK + lax.broadcasted_iota(jnp.int32, (TOK, TOK), 0)
        bias[c] = jnp.where((key >= start) & (key <= query), 0.0, NEG)


def stacked(ref, kv):
    at = kv * GROUP
    return jnp.concatenate(
        [ref[:, (at + h) * HEAD_SIZE : (at + h + 1) * HEAD_SIZE] for h in range(GROUP)], axis=0
    )


def copies(sems, pairs):
    started = [pltpu.make_async_copy(a, b, sems.at[i]) for i, (a, b) in enumerate(pairs)]
    for one in started:
        one.start()
    return started


def wait(started):
    for one in started:
        one.wait()


def rows(c):
    return pl.ds(c * TOK, TOK)


def prep_kernel(len_ref, ten_ref, x_ref, d_ref, u_ref, o_ref, low_ref, delta_ref):
    me = lax.axis_index("seq")
    low = dot(x_ref[...], d_ref[...])
    _, tenant = doc_rows(len_ref, ten_ref, chunk_positions(me))
    low_ref[...] = fold(low.T, tenant).astype(BF16)
    for h in range(delta_ref.shape[1] // TOK):
        lanes = slice(h * 128, (h + 1) * 128)
        product = u_ref[:, lanes].astype(F32) * o_ref[:, lanes].astype(F32)
        delta_ref[:, lanes] = jnp.sum(product.T, axis=0, keepdims=True)


def biased(bias, c, weights, at):
    b = bias[c]
    return weights[rows(c), at : at + 256] + jnp.concatenate([b, b], axis=1)


def blocks(parts, whole):
    out, first = [], 0
    for part in parts:
        out.append((part.at[:, pl.ds(0, whole.shape[1])], whole.at[pl.ds(first, part.shape[0])]))
        first += part.shape[0]
    return out


def values_kernel(len_ref, ten_ref, up_ref, low_ref, q_hbm, u_hbm, *refs):
    k_hbm, refs = refs[:CHUNKS], refs[CHUNKS:]
    dv_hbm, far_hbm, middle_hbm, near_hbm, last_hbm, slots_ref, top_ref, inverse_ref, *refs = refs
    q_ref, u_ref, k_ref, dv_ref, bias, weights, probs, sems = refs
    started = copies(sems, [(q_hbm, q_ref), (u_hbm, u_ref)] + blocks(k_hbm, k_ref))
    me = lax.axis_index("seq")
    fill_bias(len_ref, ten_ref, me, bias)
    wait(started)
    for kv in range(KV_HEADS):
        lanes = slice(kv * HEAD_SIZE, (kv + 1) * HEAD_SIZE)
        weights[...] = dot_nt(k_ref[:, lanes], stacked(q_ref, kv))
        for at in range(0, GROUP * TOK, 256):
            top = jnp.full((8, 256), NEG, F32)
            for c in range(CHUNKS):
                s = biased(bias, c, weights, at)
                weights[rows(c), at : at + 256] = s
                top = jnp.maximum(top, jnp.max(s.reshape(16, 8, 256), axis=0))
            top = jnp.max(top, axis=0, keepdims=True)
            total = jnp.zeros((8, 256), F32)
            for c in range(CHUNKS):
                e = jnp.exp2((weights[rows(c), at : at + 256] - top) * LOG2E_SCALE)
                weights[rows(c), at : at + 256] = e
                total = total + jnp.sum(e.reshape(16, 8, 256), axis=0)
            inverse = 1.0 / jnp.sum(total, axis=0, keepdims=True)
            for c in range(CHUNKS):
                probs[rows(c), at : at + 256] = (
                    weights[rows(c), at : at + 256] * inverse
                ).astype(BF16)
            wide = kv * GROUP * TOK + at
            top_ref[:, wide : wide + 256] = top
            inverse_ref[:, wide : wide + 256] = inverse
        dv_ref[:, lanes] = dot(probs[...], stacked(u_ref, kv)).astype(BF16)
    homes = [(far_hbm, (4, 5, 6, 7)), (middle_hbm, (2, 3)), (near_hbm, (0, 1)), (last_hbm, (8,))]
    out = copies(
        sems,
        [(dv_ref, dv_hbm)]
        + [(dv_ref.at[rows(c)], home.at[rows(n)]) for home, cs in homes for n, c in enumerate(cs)],
    )
    for j in range(SLOTS):
        slots_ref[j, :ADAPTER_RANK] = jnp.zeros((ADAPTER_RANK, TOK), BF16)
        slots_ref[j, ADAPTER_RANK:] = low_ref[...]
    for c in range(CHUNKS):
        _, tenant = doc_rows(len_ref, ten_ref, chunk_positions(me - c))
        back = dot_nt(up_ref[...], dv_ref[rows(c), :]) * adapter_scale
        owner = lax.rem(me - c + SLOTS, SLOTS)
        slots_ref[owner, :ADAPTER_RANK] = fold(back, tenant).astype(BF16)
    wait(out)


def keys_kernel(half, len_ref, ten_ref, top_ref, inverse_ref, delta_ref, q_hbm, u_hbm, *refs):
    k_hbm, refs = refs[:CHUNKS], refs[CHUNKS:]
    v_hbm, refs = refs[:3], refs[3:]
    before, refs = (refs[:3], refs[3:]) if half else ((), refs)
    n_out = 5 if half else 3
    out_hbm, refs = refs[:n_out], refs[n_out:]
    q_ref, u_ref, k_ref, v_ref, dq_ref, dk_ref, dv_ref, bias, weights, dprobs, dscores, sems = refs
    kv_width, q_width = k_ref.shape[1] // 2, q_ref.shape[1] // 2
    kv_lanes, q_lanes = pl.ds(half * kv_width, kv_width), pl.ds(half * q_width, q_width)
    me = lax.axis_index("seq")
    moves = [(ref.at[:, q_lanes], to.at[:, q_lanes]) for ref, to in ((q_hbm, q_ref), (u_hbm, u_ref))]
    moves += [(k_hbm[c].at[:, kv_lanes], k_ref.at[rows(c), kv_lanes]) for c in range(CHUNKS)]
    moves += [(a.at[:, kv_lanes], b.at[:, kv_lanes]) for a, b in blocks(v_hbm, v_ref)]
    if half:
        dv_hbm, dq_hbm, dk_hbm = before
        left = pl.ds(0, kv_width)
        moves += [
            (dv_hbm, dv_ref),
            (dq_hbm, dq_ref.at[:, pl.ds(0, q_width)]),
            (dk_hbm.at[pl.ds(0, 4 * TOK)], dk_ref.at[pl.ds(0, 4 * TOK), left]),
            (dk_hbm.at[rows(BACK)], dk_ref.at[rows(BACK), left]),
        ]
    started = copies(sems, moves)
    fill_bias(len_ref, ten_ref, me, bias)
    wait(started)
    for kv in range(half * KV_HEADS // 2, (half + 1) * KV_HEADS // 2):
        lanes = slice(kv * HEAD_SIZE, (kv + 1) * HEAD_SIZE)
        queries, upstream = stacked(q_ref, kv), stacked(u_ref, kv)
        weights[...] = dot_nt(k_ref[:, lanes], queries)
        dprobs[...] = dot_nt(v_ref[:, lanes], upstream)
        for at in range(0, GROUP * TOK, 256):
            wide = kv * GROUP * TOK + at
            top = top_ref[:, wide : wide + 256]
            inverse = inverse_ref[:, wide : wide + 256]
            delta = delta_ref[:, wide : wide + 256]
            for c in range(CHUNKS):
                s = biased(bias, c, weights, at)
                prob = jnp.exp2((s - top) * LOG2E_SCALE) * inverse
                dprob = dprobs[rows(c), at : at + 256]
                dscores[rows(c), at : at + 256] = (prob * (dprob - delta)).astype(BF16)
        dk_ref[:, lanes] = (dot(dscores[...], queries) * SCALE).astype(BF16)
        key_t = k_ref[:, lanes].astype(F32).T.astype(BF16)
        dq = dot(key_t, dscores[...]) * SCALE
        for h in range(GROUP):
            at = (kv * GROUP + h) * HEAD_SIZE
            dq_ref[:, at : at + HEAD_SIZE] = dq[:, h * TOK : (h + 1) * TOK].T.astype(BF16)
    far = dk_ref.at[pl.ds(4 * TOK, 4 * TOK), kv_lanes]
    if half:
        dq_hbm, near_hbm, middle_hbm, far_hbm, last_hbm = out_hbm
        out = [
            (dq_ref, dq_hbm),
            (dk_ref.at[pl.ds(0, 2 * TOK)], near_hbm),
            (dk_ref.at[pl.ds(2 * TOK, 2 * TOK)], middle_hbm),
            (far, far_hbm),
            (dk_ref.at[rows(BACK)], last_hbm.at[:, pl.ds(0, 2 * kv_width)]),
            (dv_ref, last_hbm.at[:, pl.ds(2 * kv_width, 2 * kv_width)]),
        ]
    else:
        dq_hbm, dk_hbm, far_hbm = out_hbm
        out = [
            (dq_ref.at[:, q_lanes], dq_hbm),
            (dk_ref.at[:, kv_lanes], dk_hbm),
            (far, far_hbm),
        ]
    wait(copies(sems, out))


def maps_kernel(len_ref, ten_ref, slots_ref, dv_hbm, x_hbm, keep_ref, send_ref, x_ref, dv_ref, sems):
    started = copies(sems, [(x_hbm, x_ref), (dv_hbm, dv_ref)])
    me = lax.axis_index("seq")
    core = lax.rem(lax.axis_index("grp"), 2)
    total = jnp.zeros((ADAPTER_RANK, TOK), F32)
    for j in range(SLOTS):
        total = total + slots_ref[j, :ADAPTER_RANK].astype(F32)
    low = []
    for c in range(CHUNKS):
        owner = lax.rem(me - c + SLOTS, SLOTS)
        _, tenant = doc_rows(len_ref, ten_ref, chunk_positions(me - c))
        low.append(expand(slots_ref[owner, ADAPTER_RANK:].astype(F32), tenant).astype(BF16))
    _, tenant = doc_rows(len_ref, ten_ref, chunk_positions(me))
    back = expand(total, tenant).astype(BF16)
    half = keep_ref.shape[1]
    width = x_ref.shape[1]
    wait(started)
    upart = (dot(jnp.concatenate(low, axis=1), dv_ref[...]) * adapter_scale).astype(BF16)

    def halves(first, second):
        first[...] = dot(back, x_ref[:, :half]).astype(BF16)
        second[:, : width - half] = dot(back, x_ref[:, half:]).astype(BF16)
        second[:, width - half :] = upart

    pl.when(core == 0)(lambda: halves(keep_ref, send_ref))
    pl.when(core == 1)(lambda: halves(send_ref, keep_ref))


def final_kernel(mine_ref, other_ref, down_ref, up_ref):
    core = lax.rem(lax.axis_index("grp"), 2)
    half = mine_ref.shape[1]
    width = down_ref.shape[0]

    def write(first, second):
        for at in range(0, width, 128):
            ref, base = (first, at) if at < half else (second, at - half)
            down_ref[at : at + 128, :] = ref[:, base : base + 128].astype(F32).T
        up_ref[...] = second[:, width - half :].astype(F32)

    pl.when(core == 0)(lambda: write(mine_ref, other_ref))
    pl.when(core == 1)(lambda: write(other_ref, mine_ref))


S, V, H = pltpu.SMEM, pltpu.VMEM, pltpu.HBM


def call(kernel, ins, outs, scratch=(), products=0, exps=0, moved=0):
    return pl.pallas_call(
        kernel,
        out_shape=tuple(jax.ShapeDtypeStruct(dims, dtype) for _, dims, dtype in outs),
        in_specs=[pl.BlockSpec(memory_space=m) for m in ins],
        out_specs=tuple(pl.BlockSpec(memory_space=m) for m, _, _ in outs),
        scratch_shapes=list(scratch),
        compiler_params=pltpu.CompilerParams(vmem_limit_bytes=VMEM_LIMIT),
        cost_estimate=pl.CostEstimate(flops=2 * products, transcendentals=exps, bytes_accessed=moved),
    )


def shifted(array, by):
    return lax.ppermute(array, "seq", [(i, (i + by) % SLOTS) for i in range(SLOTS)])


def swap(array, distance):
    count = lax.axis_size("grp")
    return lax.ppermute(array, "grp", [(i, i ^ distance) for i in range(count)])


def spread(array):
    return lax.all_to_all(array, "seq", split_axis=0, concat_axis=0, tiled=True)


def add(*arrays):
    return functools.reduce(jnp.add, [a.astype(F32) for a in arrays])


def after(array, *others):
    return lax.optimization_barrier((array,) + others)[0]


def per_device(
    inputs,
    queries,
    keys,
    values,
    outputs,
    upstream,
    lengths,
    tenants,
    adapter_down_maps,
    adapter_up_maps,
):
    x, q, k, v, o, u = (a[0] for a in (inputs, queries, keys, values, outputs, upstream))
    width, kv_width, q_width = x.shape[1], k.shape[1], q.shape[1]
    half = (width + kv_width) // 2
    ranks = TENANTS * ADAPTER_RANK
    tables = (lengths, tenants)
    work = CHUNKS * TOK * q_width
    row = (V, (1, q_width), F32)
    span = (CHUNKS * TOK, GROUP * TOK)
    bias = V((CHUNKS, TOK, TOK), F32)

    def array(chunks, lanes=kv_width):
        return (H, (chunks * TOK, lanes), BF16)

    low, delta = call(
        prep_kernel,
        [S, S] + [V] * 4,
        [(V, (ADAPTER_RANK, TOK), BF16), row],
        products=16 * work * HEAD_SIZE,
        moved=8 * work,
    )(*tables, x, adapter_down_maps, u, o)
    kv_1 = shifted(jnp.concatenate([k, v], axis=1), 1)
    k_chunks = [k, kv_1] + [shifted(k, s) for s in range(2, CHUNKS)]
    v_home = v
    v_8 = shifted(v_home, 8)
    v_01 = jnp.concatenate([v_home, kv_1[:, kv_width:]], axis=0)
    v_23 = shifted(v_01, 2)

    dv_parts, dv_far, dv_middle, dv_near, dv_last, slots, top, inverse = call(
        values_kernel,
        [S, S, V, V, H, H] + [H] * CHUNKS,
        [
            array(CHUNKS),
            array(4),
            array(2),
            array(2),
            array(1),
            (V, (SLOTS, 2 * ADAPTER_RANK, TOK), BF16),
            row,
            row,
        ],
        [
            V(q.shape, BF16),
            V(u.shape, BF16),
            V((CHUNKS * TOK, kv_width), BF16),
            V((CHUNKS * TOK, kv_width), BF16),
            bias,
            V(span, F32),
            V(span, BF16),
            pltpu.SemaphoreType.DMA((2 + CHUNKS,)),
        ],
        32 * work * HEAD_SIZE,
        work,
        12 * work,
    )(*tables, adapter_up_maps, low, q, u, *k_chunks)
    v_0123 = after(jnp.concatenate([v_01, v_23], axis=0), slots)
    v_4567 = shifted(v_0123, 4)
    slots = spread(after(slots, v_23))
    keep, send = call(
        maps_kernel,
        [S, S, V, H, H],
        [(V, (ranks, half), BF16)] * 2,
        [
            V(x.shape, BF16),
            V((CHUNKS * TOK, kv_width), BF16),
            pltpu.SemaphoreType.DMA((2,)),
        ],
    )(*tables, after(slots, v_4567, v_8), dv_parts, x)
    dv_far = shifted(dv_far, -4)
    got = swap(send, 1)
    mixed = (keep.astype(F32) + got.astype(F32)).astype(BF16)
    mixed = after(mixed.reshape(SLOTS, ranks // SLOTS, half), v_4567, v_8)
    mixed = spread(mixed)
    total = jnp.sum(mixed.astype(F32), axis=0)

    def keys_half(half, outs, *before):
        return call(
            functools.partial(keys_kernel, half),
            [S, S, V, V, V, H, H] + [H] * (CHUNKS + 3 + len(before)),
            outs,
            [
                V(q.shape, BF16),
                V(u.shape, BF16),
                V((CHUNKS * TOK, kv_width), BF16),
                V((CHUNKS * TOK, kv_width), BF16),
                V(q.shape, BF16),
                V((CHUNKS * TOK, kv_width), BF16),
                V(v.shape, BF16),
                bias,
                V(span, F32),
                V(span, F32),
                V(span, BF16),
                pltpu.SemaphoreType.DMA((2 + CHUNKS + 3 + 4,)),
            ],
            32 * work * HEAD_SIZE,
            work,
            12 * work,
        )(*tables, top, inverse, delta, q, u, *k_chunks, v_0123, v_4567, v_8, *before)

    wide = kv_width // 2
    dq, dk, far_a = keys_half(
        0, [(H, (TOK, q_width // 2), BF16), array(CHUNKS, wide), array(4, wide)]
    )
    far_a = shifted(far_a, -4)
    dq, near, middle, far_b, last = keys_half(
        1,
        [(H, q.shape, BF16), array(2), array(2), array(4, wide), array(1, 2 * kv_width)],
        dv_last,
        dq,
        dk,
    )
    far_b, last = shifted(far_b, -4), shifted(last, -8)
    far = jnp.concatenate([far_a, far_b], axis=1)

    two = 2 * TOK
    middle = shifted(add(middle, far[two:]).astype(BF16), -2)
    dv_middle = shifted(add(dv_middle, dv_far[two:]).astype(BF16), -2)
    near = add(near, far[:two], middle)
    dv_near = add(dv_near, dv_far[:two], dv_middle)
    near_out = shifted(near[TOK:].astype(BF16), -1)
    dv_out = shifted(dv_near[TOK:].astype(BF16), -1)
    keys_gradient = add(near[:TOK], near_out, last[:, :kv_width]).astype(BF16)
    values_gradient = add(dv_near[:TOK], dv_out, last[:, kv_width:]).astype(BF16)

    beside = {2: (dq, far_a, dv_far), 8: (far_b, dv_middle)}
    distance = 2
    while distance < lax.axis_size("grp"):
        short = after(total.astype(BF16), *beside.get(distance, ()))
        total = short.astype(F32) + swap(short, distance).astype(F32)
        distance *= 2
    total = after(total.astype(BF16), middle)
    mine = spread(jnp.broadcast_to(total[None], (SLOTS, ranks // SLOTS, half)))
    mine = mine.reshape(ranks, half)
    other = swap(after(mine, near_out, dv_out, last), 1)
    down, up = call(
        final_kernel, [V, V], [(V, (width, ranks), F32), (V, (ranks, kv_width), F32)]
    )(mine, other)
    return dq[None], keys_gradient[None], values_gradient[None], down, up


def solution(mesh):
    in_specs = (
        P("grp", "seq", None),
        P("grp", "seq", None),
        P("grp", "seq", None),
        P("grp", "seq", None),
        P("grp", "seq", None),
        P("grp", "seq", None),
        P("grp", None),
        P("grp", None),
        P(),
        P(),
    )
    out_specs = (P("grp", "seq", None), P("grp", "seq", None), P("grp", "seq", None), P(), P())
    return jax.shard_map(
        per_device, mesh=mesh, in_specs=in_specs, out_specs=out_specs, check_vma=False
    )
```

```python
import functools
import math

import jax
import jax.numpy as jnp
from jax import lax
from jax.experimental import pallas as pl
from jax.experimental.pallas import tpu as pltpu
from jax.sharding import PartitionSpec as P

HEAD_SIZE = 128
ADAPTER_RANK = 16
TENANTS = 8
DOCS = 8
SLOTS = 16
TOK = 128
BACK = 8
CHUNKS = BACK + 1
KV_HEADS = 4
GROUP = 8
SCALE = HEAD_SIZE**-0.5
LOG2E_SCALE = SCALE * math.log2(math.e)
NEG = -1e30
F32 = jnp.float32
BF16 = jnp.bfloat16
VMEM_LIMIT = 60 * 1024 * 1024

adapter_scale = 2.0


def dot_nt(a, b):
    return lax.dot_general(a, b, (((1,), (1,)), ((), ())), preferred_element_type=F32)


def dot(a, b):
    return jnp.dot(a, b, preferred_element_type=F32)


def doc_rows(len_ref, ten_ref, pos):
    begin = jnp.int32(0)
    start = jnp.zeros_like(pos)
    tenant = jnp.zeros_like(pos)
    for d in range(DOCS):
        inside = pos >= begin
        start = jnp.where(inside, begin, start)
        tenant = jnp.where(inside, ten_ref[0, d], tenant)
        begin = begin + len_ref[0, d]
    return start, tenant


def chunk_positions(chunk):
    return chunk * TOK + lax.broadcasted_iota(jnp.int32, (1, TOK), 1)


def fold(full, tenant):
    out = jnp.zeros((ADAPTER_RANK, TOK), F32)
    for t in range(TENANTS):
        out = out + jnp.where(tenant == t, full[t * ADAPTER_RANK : (t + 1) * ADAPTER_RANK], 0.0)
    return out


def expand(rows, tenant):
    return jnp.concatenate([jnp.where(tenant == t, rows, 0.0) for t in range(TENANTS)], axis=0)


def fill_bias(len_ref, ten_ref, me, bias):
    query = chunk_positions(me)
    start, _ = doc_rows(len_ref, ten_ref, query)
    for c in range(CHUNKS):
        key = (me - c) * TOK + lax.broadcasted_iota(jnp.int32, (TOK, TOK), 0)
        bias[c] = jnp.where((key >= start) & (key <= query), 0.0, NEG)


def stacked(ref, kv):
    at = kv * GROUP
    return jnp.concatenate(
        [ref[:, (at + h) * HEAD_SIZE : (at + h + 1) * HEAD_SIZE] for h in range(GROUP)], axis=0
    )


def copies(sems, pairs):
    started = [pltpu.make_async_copy(a, b, sems.at[i]) for i, (a, b) in enumerate(pairs)]
    for one in started:
        one.start()
    return started


def wait(started):
    for one in started:
        one.wait()


def rows(c):
    return pl.ds(c * TOK, TOK)


def prep_kernel(len_ref, ten_ref, x_ref, d_ref, u_ref, o_ref, low_ref, delta_ref):
    me = lax.axis_index("seq")
    low = dot(x_ref[...], d_ref[...])
    _, tenant = doc_rows(len_ref, ten_ref, chunk_positions(me))
    low_ref[...] = fold(low.T, tenant).astype(BF16)
    for h in range(delta_ref.shape[1] // TOK):
        lanes = slice(h * 128, (h + 1) * 128)
        product = u_ref[:, lanes].astype(F32) * o_ref[:, lanes].astype(F32)
        delta_ref[:, lanes] = jnp.sum(product.T, axis=0, keepdims=True)


def biased(bias, c, weights, at):
    b = bias[c]
    return weights[rows(c), at : at + 256] + jnp.concatenate([b, b], axis=1)


def blocks(parts, whole):
    out, first = [], 0
    for part in parts:
        out.append((part.at[:, pl.ds(0, whole.shape[1])], whole.at[pl.ds(first, part.shape[0])]))
        first += part.shape[0]
    return out


def values_kernel(len_ref, ten_ref, up_ref, low_ref, q_hbm, u_hbm, *refs):
    k_hbm, refs = refs[:CHUNKS], refs[CHUNKS:]
    dv_hbm, far_hbm, middle_hbm, near_hbm, last_hbm, slots_ref, top_ref, inverse_ref, *refs = refs
    q_ref, u_ref, k_ref, dv_ref, bias, weights, probs, sems = refs
    started = copies(sems, [(q_hbm, q_ref), (u_hbm, u_ref)] + blocks(k_hbm, k_ref))
    me = lax.axis_index("seq")
    fill_bias(len_ref, ten_ref, me, bias)
    wait(started)
    for kv in range(KV_HEADS):
        lanes = slice(kv * HEAD_SIZE, (kv + 1) * HEAD_SIZE)
        weights[...] = dot_nt(k_ref[:, lanes], stacked(q_ref, kv))
        for at in range(0, GROUP * TOK, 256):
            top = jnp.full((8, 256), NEG, F32)
            for c in range(CHUNKS):
                s = biased(bias, c, weights, at)
                weights[rows(c), at : at + 256] = s
                top = jnp.maximum(top, jnp.max(s.reshape(16, 8, 256), axis=0))
            top = jnp.max(top, axis=0, keepdims=True)
            total = jnp.zeros((8, 256), F32)
            for c in range(CHUNKS):
                e = jnp.exp2((weights[rows(c), at : at + 256] - top) * LOG2E_SCALE)
                weights[rows(c), at : at + 256] = e
                total = total + jnp.sum(e.reshape(16, 8, 256), axis=0)
            inverse = 1.0 / jnp.sum(total, axis=0, keepdims=True)
            for c in range(CHUNKS):
                probs[rows(c), at : at + 256] = (
                    weights[rows(c), at : at + 256] * inverse
                ).astype(BF16)
            wide = kv * GROUP * TOK + at
            top_ref[:, wide : wide + 256] = top
            inverse_ref[:, wide : wide + 256] = inverse
        dv_ref[:, lanes] = dot(probs[...], stacked(u_ref, kv)).astype(BF16)
    homes = [(far_hbm, (4, 5, 6, 7)), (middle_hbm, (2, 3)), (near_hbm, (0, 1)), (last_hbm, (8,))]
    out = copies(
        sems,
        [(dv_ref, dv_hbm)]
        + [(dv_ref.at[rows(c)], home.at[rows(n)]) for home, cs in homes for n, c in enumerate(cs)],
    )
    for j in range(SLOTS):
        slots_ref[j, :ADAPTER_RANK] = jnp.zeros((ADAPTER_RANK, TOK), BF16)
        slots_ref[j, ADAPTER_RANK:] = low_ref[...]
    for c in range(CHUNKS):
        _, tenant = doc_rows(len_ref, ten_ref, chunk_positions(me - c))
        back = dot_nt(up_ref[...], dv_ref[rows(c), :]) * adapter_scale
        owner = lax.rem(me - c + SLOTS, SLOTS)
        slots_ref[owner, :ADAPTER_RANK] = fold(back, tenant).astype(BF16)
    wait(out)


def keys_kernel(half, len_ref, ten_ref, top_ref, inverse_ref, delta_ref, q_hbm, u_hbm, *refs):
    k_hbm, refs = refs[:CHUNKS], refs[CHUNKS:]
    v_hbm, refs = refs[:3], refs[3:]
    before, refs = (refs[:3], refs[3:]) if half else ((), refs)
    n_out = 5 if half else 3
    out_hbm, refs = refs[:n_out], refs[n_out:]
    q_ref, u_ref, k_ref, v_ref, dq_ref, dk_ref, dv_ref, bias, weights, dprobs, dscores, sems = refs
    kv_width, q_width = k_ref.shape[1] // 2, q_ref.shape[1] // 2
    kv_lanes, q_lanes = pl.ds(half * kv_width, kv_width), pl.ds(half * q_width, q_width)
    me = lax.axis_index("seq")
    moves = [(ref.at[:, q_lanes], to.at[:, q_lanes]) for ref, to in ((q_hbm, q_ref), (u_hbm, u_ref))]
    moves += [(k_hbm[c].at[:, kv_lanes], k_ref.at[rows(c), kv_lanes]) for c in range(CHUNKS)]
    moves += [(a.at[:, kv_lanes], b.at[:, kv_lanes]) for a, b in blocks(v_hbm, v_ref)]
    if half:
        dv_hbm, dq_hbm, dk_hbm = before
        left = pl.ds(0, kv_width)
        moves += [
            (dv_hbm, dv_ref),
            (dq_hbm, dq_ref.at[:, pl.ds(0, q_width)]),
            (dk_hbm.at[pl.ds(0, 4 * TOK)], dk_ref.at[pl.ds(0, 4 * TOK), left]),
            (dk_hbm.at[rows(BACK)], dk_ref.at[rows(BACK), left]),
        ]
    started = copies(sems, moves)
    fill_bias(len_ref, ten_ref, me, bias)
    wait(started)
    for kv in range(half * KV_HEADS // 2, (half + 1) * KV_HEADS // 2):
        lanes = slice(kv * HEAD_SIZE, (kv + 1) * HEAD_SIZE)
        queries, upstream = stacked(q_ref, kv), stacked(u_ref, kv)
        weights[...] = dot_nt(k_ref[:, lanes], queries)
        dprobs[...] = dot_nt(v_ref[:, lanes], upstream)
        for at in range(0, GROUP * TOK, 256):
            wide = kv * GROUP * TOK + at
            top = top_ref[:, wide : wide + 256]
            inverse = inverse_ref[:, wide : wide + 256]
            delta = delta_ref[:, wide : wide + 256]
            for c in range(CHUNKS):
                s = biased(bias, c, weights, at)
                prob = jnp.exp2((s - top) * LOG2E_SCALE) * inverse
                dprob = dprobs[rows(c), at : at + 256]
                dscores[rows(c), at : at + 256] = (prob * (dprob - delta)).astype(BF16)
        dk_ref[:, lanes] = (dot(dscores[...], queries) * SCALE).astype(BF16)
        key_t = k_ref[:, lanes].astype(F32).T.astype(BF16)
        dq = dot(key_t, dscores[...]) * SCALE
        for h in range(GROUP):
            at = (kv * GROUP + h) * HEAD_SIZE
            dq_ref[:, at : at + HEAD_SIZE] = dq[:, h * TOK : (h + 1) * TOK].T.astype(BF16)
    far = dk_ref.at[pl.ds(4 * TOK, 4 * TOK), kv_lanes]
    if half:
        dq_hbm, near_hbm, middle_hbm, far_hbm, last_hbm = out_hbm
        out = [
            (dq_ref, dq_hbm),
            (dk_ref.at[pl.ds(0, 2 * TOK)], near_hbm),
            (dk_ref.at[pl.ds(2 * TOK, 2 * TOK)], middle_hbm),
            (far, far_hbm),
            (dk_ref.at[rows(BACK)], last_hbm.at[:, pl.ds(0, 2 * kv_width)]),
            (dv_ref, last_hbm.at[:, pl.ds(2 * kv_width, 2 * kv_width)]),
        ]
    else:
        dq_hbm, dk_hbm, far_hbm = out_hbm
        out = [
            (dq_ref.at[:, q_lanes], dq_hbm),
            (dk_ref.at[:, kv_lanes], dk_hbm),
            (far, far_hbm),
        ]
    wait(copies(sems, out))


def maps_kernel(len_ref, ten_ref, slots_ref, dv_hbm, x_hbm, keep_ref, send_ref, x_ref, dv_ref, sems):
    started = copies(sems, [(x_hbm, x_ref), (dv_hbm, dv_ref)])
    me = lax.axis_index("seq")
    core = lax.rem(lax.axis_index("grp"), 2)
    total = jnp.zeros((ADAPTER_RANK, TOK), F32)
    for j in range(SLOTS):
        total = total + slots_ref[j, :ADAPTER_RANK].astype(F32)
    low = []
    for c in range(CHUNKS):
        owner = lax.rem(me - c + SLOTS, SLOTS)
        _, tenant = doc_rows(len_ref, ten_ref, chunk_positions(me - c))
        low.append(expand(slots_ref[owner, ADAPTER_RANK:].astype(F32), tenant).astype(BF16))
    _, tenant = doc_rows(len_ref, ten_ref, chunk_positions(me))
    back = expand(total, tenant).astype(BF16)
    half = keep_ref.shape[1]
    width = x_ref.shape[1]
    wait(started)
    upart = (dot(jnp.concatenate(low, axis=1), dv_ref[...]) * adapter_scale).astype(BF16)

    def halves(first, second):
        first[...] = dot(back, x_ref[:, :half]).astype(BF16)
        second[:, : width - half] = dot(back, x_ref[:, half:]).astype(BF16)
        second[:, width - half :] = upart

    pl.when(core == 0)(lambda: halves(keep_ref, send_ref))
    pl.when(core == 1)(lambda: halves(send_ref, keep_ref))


def final_kernel(mine_ref, other_ref, down_ref, up_ref):
    core = lax.rem(lax.axis_index("grp"), 2)
    half = mine_ref.shape[1]
    width = down_ref.shape[0]

    def write(first, second):
        for at in range(0, width, 128):
            ref, base = (first, at) if at < half else (second, at - half)
            down_ref[at : at + 128, :] = ref[:, base : base + 128].astype(F32).T
        up_ref[...] = second[:, width - half :].astype(F32)

    pl.when(core == 0)(lambda: write(mine_ref, other_ref))
    pl.when(core == 1)(lambda: write(other_ref, mine_ref))


S, V, H = pltpu.SMEM, pltpu.VMEM, pltpu.HBM


def call(kernel, ins, outs, scratch=(), products=0, exps=0, moved=0):
    return pl.pallas_call(
        kernel,
        out_shape=tuple(jax.ShapeDtypeStruct(dims, dtype) for _, dims, dtype in outs),
        in_specs=[pl.BlockSpec(memory_space=m) for m in ins],
        out_specs=tuple(pl.BlockSpec(memory_space=m) for m, _, _ in outs),
        scratch_shapes=list(scratch),
        compiler_params=pltpu.CompilerParams(vmem_limit_bytes=VMEM_LIMIT),
        cost_estimate=pl.CostEstimate(flops=2 * products, transcendentals=exps, bytes_accessed=moved),
    )


def shifted(array, by):
    return lax.ppermute(array, "seq", [(i, (i + by) % SLOTS) for i in range(SLOTS)])


def swap(array, distance):
    count = lax.axis_size("grp")
    return lax.ppermute(array, "grp", [(i, i ^ distance) for i in range(count)])


def spread(array):
    return lax.all_to_all(array, "seq", split_axis=0, concat_axis=0, tiled=True)


def add(*arrays):
    return functools.reduce(jnp.add, [a.astype(F32) for a in arrays])


def after(array, *others):
    return lax.optimization_barrier((array,) + others)[0]


def per_device(
    inputs,
    queries,
    keys,
    values,
    outputs,
    upstream,
    lengths,
    tenants,
    adapter_down_maps,
    adapter_up_maps,
):
    x, q, k, v, o, u = (a[0] for a in (inputs, queries, keys, values, outputs, upstream))
    width, kv_width, q_width = x.shape[1], k.shape[1], q.shape[1]
    half = (width + kv_width) // 2
    ranks = TENANTS * ADAPTER_RANK
    tables = (lengths, tenants)
    work = CHUNKS * TOK * q_width
    row = (V, (1, q_width), F32)
    span = (CHUNKS * TOK, GROUP * TOK)
    bias = V((CHUNKS, TOK, TOK), F32)

    def array(chunks, lanes=kv_width):
        return (H, (chunks * TOK, lanes), BF16)

    low, delta = call(
        prep_kernel,
        [S, S] + [V] * 4,
        [(V, (ADAPTER_RANK, TOK), BF16), row],
        products=16 * work * HEAD_SIZE,
        moved=8 * work,
    )(*tables, x, adapter_down_maps, u, o)
    kv_1 = shifted(jnp.concatenate([k, v], axis=1), 1)
    k_chunks = [k, kv_1] + [shifted(k, s) for s in range(2, CHUNKS)]
    v_home = v
    v_8 = shifted(v_home, 8)
    v_01 = jnp.concatenate([v_home, kv_1[:, kv_width:]], axis=0)
    v_23 = shifted(v_01, 2)

    dv_parts, dv_far, dv_middle, dv_near, dv_last, slots, top, inverse = call(
        values_kernel,
        [S, S, V, V, H, H] + [H] * CHUNKS,
        [
            array(CHUNKS),
            array(4),
            array(2),
            array(2),
            array(1),
            (V, (SLOTS, 2 * ADAPTER_RANK, TOK), BF16),
            row,
            row,
        ],
        [
            V(q.shape, BF16),
            V(u.shape, BF16),
            V((CHUNKS * TOK, kv_width), BF16),
            V((CHUNKS * TOK, kv_width), BF16),
            bias,
            V(span, F32),
            V(span, BF16),
            pltpu.SemaphoreType.DMA((2 + CHUNKS,)),
        ],
        32 * work * HEAD_SIZE,
        work,
        12 * work,
    )(*tables, adapter_up_maps, low, q, u, *k_chunks)
    v_0123 = after(jnp.concatenate([v_01, v_23], axis=0), slots)
    v_4567 = shifted(v_0123, 4)
    slots = spread(after(slots, v_23))
    def keys_half(half, outs, *before):
        return call(
            functools.partial(keys_kernel, half),
            [S, S, V, V, V, H, H] + [H] * (CHUNKS + 3 + len(before)),
            outs,
            [
                V(q.shape, BF16),
                V(u.shape, BF16),
                V((CHUNKS * TOK, kv_width), BF16),
                V((CHUNKS * TOK, kv_width), BF16),
                V(q.shape, BF16),
                V((CHUNKS * TOK, kv_width), BF16),
                V(v.shape, BF16),
                bias,
                V(span, F32),
                V(span, F32),
                V(span, BF16),
                pltpu.SemaphoreType.DMA((2 + CHUNKS + 3 + 4,)),
            ],
            32 * work * HEAD_SIZE,
            work,
            12 * work,
        )(*tables, top, inverse, delta, q, u, *k_chunks, v_0123, v_4567, v_8, *before)

    wide = kv_width // 2
    dq, dk, far_a = keys_half(
        0, [(H, (TOK, q_width // 2), BF16), array(CHUNKS, wide), array(4, wide)]
    )
    keep, send = call(
        maps_kernel,
        [S, S, V, H, H],
        [(V, (ranks, half), BF16)] * 2,
        [
            V(x.shape, BF16),
            V((CHUNKS * TOK, kv_width), BF16),
            pltpu.SemaphoreType.DMA((2,)),
        ],
    )(*tables, after(slots, v_4567, v_8, dk), dv_parts, x)
    dv_far = shifted(dv_far, -4)
    got = swap(send, 1)
    mixed = (keep.astype(F32) + got.astype(F32)).astype(BF16)
    mixed = after(mixed.reshape(SLOTS, ranks // SLOTS, half), v_4567, v_8)
    mixed = spread(mixed)
    total = jnp.sum(mixed.astype(F32), axis=0)

    far_a = shifted(far_a, -4)
    dq, near, middle, far_b, last = keys_half(
        1,
        [(H, q.shape, BF16), array(2), array(2), array(4, wide), array(1, 2 * kv_width)],
        dv_last,
        dq,
        dk,
    )
    far_b, last = shifted(far_b, -4), shifted(last, -8)
    far = jnp.concatenate([far_a, far_b], axis=1)

    two = 2 * TOK
    middle = shifted(add(middle, far[two:]).astype(BF16), -2)
    dv_middle = shifted(add(dv_middle, dv_far[two:]).astype(BF16), -2)
    near = add(near, far[:two], middle)
    dv_near = add(dv_near, dv_far[:two], dv_middle)
    near_out = shifted(near[TOK:].astype(BF16), -1)
    dv_out = shifted(dv_near[TOK:].astype(BF16), -1)
    keys_gradient = add(near[:TOK], near_out, last[:, :kv_width]).astype(BF16)
    values_gradient = add(dv_near[:TOK], dv_out, last[:, kv_width:]).astype(BF16)

    beside = {2: (dq, far_a, dv_far), 8: (far_b, dv_middle)}
    distance = 2
    while distance < lax.axis_size("grp"):
        short = after(total.astype(BF16), *beside.get(distance, ()))
        total = short.astype(F32) + swap(short, distance).astype(F32)
        distance *= 2
    total = after(total.astype(BF16), middle)
    mine = spread(jnp.broadcast_to(total[None], (SLOTS, ranks // SLOTS, half)))
    mine = mine.reshape(ranks, half)
    other = swap(after(mine, near_out, dv_out, last), 1)
    down, up = call(
        final_kernel, [V, V], [(V, (width, ranks), F32), (V, (ranks, kv_width), F32)]
    )(mine, other)
    return dq[None], keys_gradient[None], values_gradient[None], down, up


def solution(mesh):
    in_specs = (
        P("grp", "seq", None),
        P("grp", "seq", None),
        P("grp", "seq", None),
        P("grp", "seq", None),
        P("grp", "seq", None),
        P("grp", "seq", None),
        P("grp", None),
        P("grp", None),
        P(),
        P(),
    )
    out_specs = (P("grp", "seq", None), P("grp", "seq", None), P("grp", "seq", None), P(), P())
    return jax.shard_map(
        per_device, mesh=mesh, in_specs=in_specs, out_specs=out_specs, check_vma=False
    )
```
